1024 devices in a mesh: row: 128 (over z, x), col: 8 (over y, core).
Axes of the slice: x: 4, y: 4, z: 32, core: 2. Of those that a mesh axis runs over, the one named last changes fastest.
Arguments:
- stored_matrix: float32 [20480, 20480], P('row', 'col'), may hold values from -30 to 30, as said below
- panel_block: float32 [20480, 256], P('row'), may hold values from -70 to 70
Outputs:
- updated: float32 [20480, 20480], P('row', 'col')
The draws below stay inside these ranges and needn't reach their ends.
Inputs may be any that keep to these rules, and one draw needn't show every extreme that they name: The matrix S that stored_matrix holds is symmetric.
All inputs are finite; a program needn't handle non-finite values.
Results may differ from the reference program's by a relative error of at most 0.000073.
Values sent between devices are 32-bit elements; how exact they have to be, the bound alone decides.
No kernel may reach another device: no remote copies, remote signals or barrier semaphores. Data moves between devices by JAX's collectives and lax.ppermute only.
A program may use at most 64 MiB of HBM per device.

```python
import jax
import jax.numpy as jnp
from jax import lax

BAND = 256
FINE = 20
PROW = 128
PCOL = 8
ORDER = 20480


def draw_stored_matrix(key, part):
    key = jax.random.fold_in(key, 11)
    key_raw, key_scale = jax.random.split(key)
    raw = jnp.clip(jax.random.normal(key_raw, (ORDER, ORDER), jnp.float32), -4.0, 4.0)
    scales = jnp.exp(jax.random.uniform(key_scale, (ORDER,), jnp.float32, -1.15, 1.15))
    symmetric = (raw + raw.T) * 0.35
    symmetric = symmetric * scales[:, None] * scales[None, :]
    return symmetric.reshape(ORDER, PROW, PCOL, FINE).transpose(0, 2, 1, 3).reshape(ORDER, ORDER)


def draw_panel_block(key, part):
    key = jax.random.fold_in(key, 23)
    key_raw, key_rough, key_cols = jax.random.split(key, 3)
    ramp = 1.0 + 2.0 * jnp.arange(ORDER, dtype=jnp.float32) / (ORDER - 1)
    raw = jnp.clip(jax.random.normal(key_raw, (ORDER, BAND), jnp.float32), -4.0, 4.0)
    rough = jnp.exp(jax.random.uniform(key_rough, (ORDER,), jnp.float32, -0.5, 0.5))
    col_scales = jnp.exp(jax.random.uniform(key_cols, (BAND,), jnp.float32, -1.15, 1.15))
    return raw * (ramp * rough)[:, None] * col_scales[None, :]


def setup_inputs(seed: int = 0) -> dict:
    streams_of = jax.random.split(jax.random.key(seed), 3)
    return {
        "stored_matrix": draw_stored_matrix(jax.random.fold_in(streams_of[2], 71), 0),
        "panel_block": draw_panel_block(jax.random.fold_in(streams_of[2], 71), 0),
    }


def left_solve(factor, rhs):
    return lax.linalg.triangular_solve(factor, rhs, left_side=True, lower=True)

def to_stored(natural_rows):
    width = natural_rows.shape[1]
    return natural_rows.reshape(PROW, PCOL, FINE, width).transpose(1, 0, 2, 3).reshape(ORDER, width)

def reference(stored_matrix, panel_block):
    highest = lax.Precision.HIGHEST
    gram_term = jnp.dot(panel_block.T.astype(jnp.float32), panel_block.astype(jnp.float32), precision=highest, preferred_element_type=jnp.float32)
    factor = jnp.linalg.cholesky(gram_term)
    basis_rows = left_solve(factor, panel_block.T).T
    image_rows = jnp.dot(stored_matrix.astype(jnp.float32), to_stored(panel_block).astype(jnp.float32), precision=highest, preferred_element_type=jnp.float32)
    cross_term = jnp.dot(panel_block.T.astype(jnp.float32), image_rows.astype(jnp.float32), precision=highest, preferred_element_type=jnp.float32)
    reduced = left_solve(factor, image_rows.T).T
    core_term = left_solve(factor, left_solve(factor, cross_term).T).T
    reflector = 2.0 * reduced - 2.0 * jnp.dot(basis_rows.astype(jnp.float32), core_term.astype(jnp.float32), precision=highest, preferred_element_type=jnp.float32)
    row_factors = jnp.concatenate([basis_rows, reflector], axis=1)
    col_factors = jnp.concatenate([to_stored(reflector), to_stored(basis_rows)], axis=1)
    return stored_matrix - jnp.dot(row_factors.astype(jnp.float32), col_factors.T.astype(jnp.float32), precision=highest, preferred_element_type=jnp.float32)
```

```python
import jax
import jax.numpy as jnp
from jax import lax
from jax.experimental import pallas as pl
from jax.experimental.pallas import tpu as pltpu
from jax.sharding import Mesh, PartitionSpec as P

FINE = 20
BAND = 256
LANES = 128
HALVES = BAND // LANES
PIECE = FINE * HALVES
SLICE = BAND // 8 * HALVES
FAR, NEAR, XS, YS, CORES = 16, 2, 4, 4, 2
GROUPS = NEAR * XS
COLS = YS * CORES
VMEM = pl.BlockSpec(memory_space=pltpu.VMEM)
PARAMS = pltpu.CompilerParams(vmem_limit_bytes=48 * 1024 * 1024)


def precise(left, right, dims):
    return lax.dot_general(
        left, right, (dims, ((), ())), precision=lax.Precision.HIGHEST, preferred_element_type=jnp.float32
    )


def split(value):
    high = value.astype(jnp.bfloat16)
    return high, (value - high.astype(jnp.float32)).astype(jnp.bfloat16)


def three_pass(left, right, dims):
    (lh, ll), (rh, rl) = left, right

    def one(a, b):
        return lax.dot_general(a, b, (dims, ((), ())), preferred_element_type=jnp.float32)

    return (one(lh, rl) + one(ll, rh)) + one(lh, rh)


def stack_halves(value):
    return jnp.concatenate([value[:, i * LANES : (i + 1) * LANES] for i in range(HALVES)], axis=0)


def assemble(pieces, far, base, rows, target):
    for half in range(HALVES):
        lo = base + half * FINE
        target[rows, half * LANES : (half + 1) * LANES] = jnp.concatenate(
            [pieces[g, far, lo : lo + FINE, :] for g in range(GROUPS)], axis=0
        )


def first_kernel(stored, gathered, panel, columns, payload):
    far_rows = GROUPS * FINE

    @pl.loop(0, FAR)
    def _(far):
        assemble(gathered, far, 0, pl.ds(pl.multiple_of(far * far_rows, 8), far_rows), columns)

    wide = far_rows * 4
    image = jnp.zeros((panel.shape[0], BAND), jnp.float32)
    gram = jnp.zeros((BAND, BAND), jnp.float32)
    for i in range(stored.shape[1] // wide):
        part = columns[i * wide : (i + 1) * wide, :]
        image += three_pass(split(stored[:, i * wide : (i + 1) * wide]), split(part), ((1,), (0,)))
        gram += precise(part, part, ((0,), (0,)))
    cross = precise(panel[...], image, ((0,), (0,)))
    eighth = BAND // COLS
    for c in range(COLS):
        payload[c, :PIECE, :] = stack_halves(image[c * FINE : (c + 1) * FINE, :])
        payload[c, PIECE : PIECE + SLICE, :] = stack_halves(gram[c * eighth : (c + 1) * eighth, :])
        payload[c, PIECE + SLICE :, :] = stack_halves(cross[c * eighth : (c + 1) * eighth, :])


def eliminate(block):
    n = block.shape[0]
    row_id = lax.broadcasted_iota(jnp.int32, (n, 1), 0)
    eye = (lax.broadcasted_iota(jnp.int32, (n, n), 0) == lax.broadcasted_iota(jnp.int32, (n, n), 1)).astype(
        jnp.float32
    )
    work = jnp.concatenate([block, eye], axis=1)
    for j in range(0, n, 2):
        row0, row1 = work[j : j + 1, :], work[j + 1 : j + 2, :]
        p, b, d = row0[:, j : j + 1], row0[:, j + 1 : j + 2], row1[:, j + 1 : j + 2]
        inv0 = 1.0 / p
        inv1 = 1.0 / (d - b * (b * inv0))
        row1 = row1 - (b * inv0) * row0
        f0 = jnp.where(row_id > j + 1, work[:, j : j + 1] * inv0, 0.0)
        f1 = jnp.where(row_id > j + 1, (work[:, j + 1 : j + 2] - f0 * b) * inv1, 0.0)
        work = jnp.where(row_id == j + 1, row1, work - f0 * row0 - f1 * row1)
    pivots = jnp.sum(work[:, :n] * eye, axis=1, keepdims=True)
    return work[:, n:], pivots


def invert(gram, work):
    n, size = 64, BAND
    work[:, :size] = gram
    work[:, size:] = (
        lax.broadcasted_iota(jnp.int32, (size, size), 0) == lax.broadcasted_iota(jnp.int32, (size, size), 1)
    ).astype(jnp.float32)
    scaled = []
    for k in range(size // n):
        lo, hi = k * n, (k + 1) * n
        unit, pivots = eliminate(work[lo:hi, lo:hi])
        rows = precise(unit, work[lo:hi, :], ((1,), (0,)))
        work[lo:hi, :] = rows
        over = rows * (1.0 / pivots)
        scaled.append(over[:, size:])
        if hi < size:
            work[hi:, :] = work[hi:, :] - precise(rows[:, hi:size], over, ((0,), (0,)))
    return jnp.concatenate(scaled, axis=0)


def unstack(ref, lo, rows):
    return jnp.concatenate(
        [
            jnp.concatenate([ref[c, lo + h * rows : lo + (h + 1) * rows, :] for h in range(HALVES)], axis=1)
            for c in range(COLS)
        ],
        axis=0,
    )


def second_kernel(panel, small, left, right, work):
    eighth = BAND // COLS
    image = unstack(small, 0, FINE)
    gram = unstack(small, PIECE, eighth)
    cross = unstack(small, PIECE + SLICE, eighth)
    scaled = invert(gram, work)
    unit = work[:, BAND:]

    def by_inverse(value):
        return precise(precise(value, unit, ((1,), (1,))), scaled, ((1,), (0,)))

    first = 2.0 * by_inverse(panel[...])
    left[...] = first
    right[...] = 2.0 * by_inverse(image - precise(first, cross, ((1,), (0,))))


def third_kernel(place, stored, left, right, columns, own, *rest):
    others, (out, pieces, image) = rest[:-3], rest[-3:]
    near, x = place[0], place[1]
    for shift, block in enumerate((own, *others)):
        source = lax.rem(x - shift + XS, XS)
        for flip in range(NEAR):
            group = lax.rem(near + flip, NEAR) * XS + source
            pieces[group] = block[flip]
    far_rows = GROUPS * FINE

    @pl.loop(0, FAR)
    def _(far):
        assemble(pieces, far, 0, pl.ds(pl.multiple_of(far * far_rows, 8), far_rows), image)

    a, b = split(left[...]), split(right[...])
    wide = far_rows * 4
    for i in range(stored.shape[1] // wide):
        at = slice(i * wide, (i + 1) * wide)
        out[:, at] = stored[:, at] - (
            three_pass(a, split(image[at, :]), ((1,), (1,))) + three_pass(b, split(columns[at, :]), ((1,), (1,)))
        )


def on_device(stored, panel):
    f32 = jnp.float32
    rows, width = stored.shape
    col = ("y", "core")
    group = ("near", "x")
    c = lax.axis_index(col)
    own = stack_halves(lax.dynamic_slice_in_dim(panel, c * FINE, FINE, 0))
    far = lax.all_gather(own, "far", axis=0, tiled=True)
    gathered = lax.all_to_all(jnp.broadcast_to(far[None], (GROUPS, *far.shape)), group, 0, 0)
    pieces_shape = (GROUPS, FAR, PIECE, LANES)
    columns, payload = pl.pallas_call(
        first_kernel,
        out_shape=(
            jax.ShapeDtypeStruct((width, BAND), f32),
            jax.ShapeDtypeStruct((COLS, PIECE + 2 * SLICE, LANES), f32),
        ),
        in_specs=[VMEM] * 3,
        out_specs=(VMEM, VMEM),
        compiler_params=PARAMS,
        name="image_and_gram",
    )(stored, gathered.reshape(pieces_shape), panel)
    summed = jnp.sum(lax.all_to_all(payload, col, 0, 0), axis=0)
    image_own, gram_own, cross_own = jnp.split(summed, (PIECE, PIECE + SLICE), axis=0)

    both = lax.all_gather(jnp.concatenate([image_own, cross_own], axis=0), "far", axis=0)
    image_far = both[:, :PIECE, :]
    cross_far = jnp.sum(both[:, PIECE:, :], axis=0)
    swapped = lax.ppermute(image_far, "near", [(0, 1), (1, 0)])
    image_near = jnp.stack([image_far, swapped])
    cross_parts = lax.all_to_all(jnp.broadcast_to(cross_far[None], (GROUPS, *cross_far.shape)), group, 0, 0)
    others = [lax.ppermute(image_near, "x", [(i, (i + d) % XS) for i in range(XS)]) for d in range(1, XS)]
    cross_own = jnp.sum(cross_parts, axis=0)
    small = lax.all_gather(jnp.concatenate([image_own, gram_own, cross_own], axis=0), col, axis=0)
    left, right = pl.pallas_call(
        second_kernel,
        out_shape=(jax.ShapeDtypeStruct((rows, BAND), f32),) * 2,
        in_specs=[VMEM] * 2,
        out_specs=(VMEM, VMEM),
        scratch_shapes=[pltpu.VMEM((BAND, 2 * BAND), f32)],
        compiler_params=PARAMS,
        name="row_factors",
    )(panel, small)
    place = jnp.stack([lax.axis_index("near"), lax.axis_index("x")]).astype(jnp.int32)
    return pl.pallas_call(
        third_kernel,
        out_shape=jax.ShapeDtypeStruct((rows, width), f32),
        in_specs=[pl.BlockSpec(memory_space=pltpu.SMEM)] + [VMEM] * (4 + XS),
        out_specs=VMEM,
        scratch_shapes=[pltpu.VMEM(pieces_shape, f32), pltpu.VMEM((width, BAND), f32)],
        compiler_params=PARAMS,
        name="update",
    )(place, stored, left, right, columns, image_near, *others)


def solution(mesh):
    sizes = (FAR, NEAR, XS, YS, CORES)
    fine_mesh = Mesh(mesh.devices.reshape(sizes), ("far", "near", "x", "y", "core"))
    row, col = ("far", "near", "x"), ("y", "core")
    return jax.shard_map(
        on_device, mesh=fine_mesh, in_specs=(P(row, col), P(row, None)), out_specs=P(row, col), check_vma=False
    )
```

```python
import jax
import jax.numpy as jnp
from jax import lax
from jax.experimental import pallas as pl
from jax.experimental.pallas import tpu as pltpu
from jax.sharding import Mesh, PartitionSpec as P

FINE = 20
BAND = 256
LANES = 128
HALVES = BAND // LANES
TILE = 8
PIECE = FINE * HALVES
SLICE = BAND // 8 * HALVES
FAR, NEAR, XS, YS, CORES = 16, 2, 4, 4, 2
GROUPS = NEAR * XS
COLS = YS * CORES
VMEM = pl.BlockSpec(memory_space=pltpu.VMEM)
PARAMS = pltpu.CompilerParams(vmem_limit_bytes=48 * 1024 * 1024)


def precise(left, right, dims):
    return lax.dot_general(
        left, right, (dims, ((), ())), precision=lax.Precision.HIGHEST, preferred_element_type=jnp.float32
    )


def identity(n):
    return (lax.broadcasted_iota(jnp.int32, (n, n), 0) == lax.broadcasted_iota(jnp.int32, (n, n), 1)).astype(
        jnp.float32
    )


def split(value):
    high = value.astype(jnp.bfloat16)
    return high, (value - high.astype(jnp.float32)).astype(jnp.bfloat16)


def three_pass(left, right, dims):
    (lh, ll), (rh, rl) = left, right

    def one(a, b):
        return lax.dot_general(a, b, (dims, ((), ())), preferred_element_type=jnp.float32)

    return (one(lh, rl) + one(ll, rh)) + one(lh, rh)


def stack_halves(value):
    return jnp.concatenate([value[:, i * LANES : (i + 1) * LANES] for i in range(HALVES)], axis=0)


def assemble(pieces, far, base, rows, target):
    for half in range(HALVES):
        lo = base + half * FINE
        target[rows, half * LANES : (half + 1) * LANES] = jnp.concatenate(
            [pieces[g, far, lo : lo + FINE, :] for g in range(GROUPS)], axis=0
        )


def first_kernel(stored, gathered, panel, columns, payload):
    far_rows = GROUPS * FINE

    @pl.loop(0, FAR)
    def _(far):
        assemble(gathered, far, 0, pl.ds(pl.multiple_of(far * far_rows, 8), far_rows), columns)

    wide = far_rows * 4
    image = jnp.zeros((panel.shape[0], BAND), jnp.float32)
    gram = jnp.zeros((BAND, BAND), jnp.float32)
    for i in range(stored.shape[1] // wide):
        part = columns[i * wide : (i + 1) * wide, :]
        image += three_pass(split(stored[:, i * wide : (i + 1) * wide]), split(part), ((1,), (0,)))
        gram += precise(part, part, ((0,), (0,)))
    cross = precise(panel[...], image, ((0,), (0,)))
    eighth = BAND // COLS
    for c in range(COLS):
        payload[c, :PIECE, :] = stack_halves(image[c * FINE : (c + 1) * FINE, :])
        payload[c, PIECE : PIECE + SLICE, :] = stack_halves(gram[c * eighth : (c + 1) * eighth, :])
        payload[c, PIECE + SLICE :, :] = stack_halves(cross[c * eighth : (c + 1) * eighth, :])


def eliminate(block):
    n, wide = block.shape[0], 2 * block.shape[0]
    eye = identity(n)
    work = jnp.concatenate([block, eye], axis=1)
    tiles = [work[i : i + TILE, :] for i in range(0, n, TILE)]
    sub = lax.broadcasted_iota(jnp.int32, (TILE, wide), 0)
    for t in range(n // TILE):
        j = t * TILE
        rows = [tiles[t][k : k + 1, :] for k in range(TILE)]
        square = [
            [jnp.broadcast_to(rows[k][:, j + l : j + l + 1], (1, wide)) if l >= k else None for l in range(TILE)]
            for k in range(TILE)
        ]
        cols = [[jnp.broadcast_to(tile[:, j + k : j + k + 1], (TILE, wide)) for tile in tiles[t:]] for k in range(TILE)]
        for k in range(TILE):
            inverse = 1.0 / square[k][k]
            for m in range(k + 1, TILE):
                factor = square[k][m] * inverse
                rows[m] = rows[m] - factor * rows[k]
                for l in range(m, TILE):
                    square[m][l] = square[m][l] - factor * square[k][l]
            factors = [col * inverse for col in cols[k]]
            factors[0] = jnp.where(sub > k, factors[0], 0.0)
            for l in range(k + 1, TILE):
                cols[l] = [col - f * square[k][l] for col, f in zip(cols[l], factors)]
            for i, f in enumerate(factors):
                tiles[t + i] = tiles[t + i] - f * rows[k]
    work = jnp.concatenate(tiles, axis=0)
    return work[:, n:], jnp.sum(work[:, :n] * eye, axis=1, keepdims=True)


def invert(gram, work, scaled):
    n, size = 64, BAND
    work[:, :size] = gram
    work[:, size:] = identity(size)
    for k in range(size // n):
        lo, hi = k * n, (k + 1) * n
        unit, pivots = eliminate(work[lo:hi, lo:hi])
        rows = precise(unit, work[lo:hi, lo : size + hi], ((1,), (0,)))
        work[lo:hi, lo : size + hi] = rows
        over = rows * (1.0 / pivots)
        scaled[lo:hi, :] = jnp.zeros((n, size), jnp.float32)
        scaled[lo:hi, :hi] = over[:, size - lo :]
        if hi < size:
            work[hi:, hi : size + hi] = work[hi:, hi : size + hi] - precise(
                rows[:, n : size - lo], over[:, n:], ((0,), (0,))
            )


def unstack(ref, lo, rows):
    return jnp.concatenate(
        [
            jnp.concatenate([ref[c, lo + h * rows : lo + (h + 1) * rows, :] for h in range(HALVES)], axis=1)
            for c in range(COLS)
        ],
        axis=0,
    )


def by_inverse(value, unit, scaled):
    return precise(precise(value, unit, ((1,), (1,))), scaled, ((1,), (0,)))


def second_kernel(panel, small, unit, scaled, left, work):
    invert(unstack(small, PIECE, BAND // COLS), work, scaled)
    unit[...] = work[:, BAND:]
    left[...] = 2.0 * by_inverse(panel[...], unit[...], scaled[...])


def third_kernel(stored, left, unit, scaled, small, columns, pieces, out, image):
    far_rows = GROUPS * FINE

    @pl.loop(0, FAR)
    def _(far):
        assemble(pieces, far, 0, pl.ds(pl.multiple_of(far * far_rows, 8), far_rows), image)

    cross = unstack(small, PIECE + SLICE, BAND // COLS)
    own = unstack(small, 0, FINE) - precise(left[...], cross, ((1,), (0,)))
    a, b = split(left[...]), split(2.0 * by_inverse(own, unit[...], scaled[...]))
    wide = far_rows * 4
    for i in range(stored.shape[1] // wide):
        at = slice(i * wide, (i + 1) * wide)
        out[:, at] = stored[:, at] - (
            three_pass(a, split(image[at, :]), ((1,), (1,))) + three_pass(b, split(columns[at, :]), ((1,), (1,)))
        )


def spread(value, axes, count):
    return lax.all_to_all(jnp.broadcast_to(value[None], (count, *value.shape)), axes, 0, 0)


def on_device(stored, panel):
    f32 = jnp.float32
    rows, width = stored.shape
    col = ("y", "core")
    group = ("near", "x")
    c = lax.axis_index(col)
    pieces_shape = (GROUPS, FAR, PIECE, LANES)
    own = stack_halves(lax.dynamic_slice_in_dim(panel, c * FINE, FINE, 0))
    gathered = spread(lax.all_gather(own, "far", axis=0), group, GROUPS)
    columns, payload = pl.pallas_call(
        first_kernel,
        out_shape=(
            jax.ShapeDtypeStruct((width, BAND), f32),
            jax.ShapeDtypeStruct((COLS, PIECE + 2 * SLICE, LANES), f32),
        ),
        in_specs=[VMEM] * 3,
        out_specs=(VMEM, VMEM),
        compiler_params=PARAMS,
        name="image_and_gram",
    )(stored, gathered, panel)
    summed = jnp.sum(lax.all_to_all(payload, col, 0, 0), axis=0)
    far = lax.all_gather(jnp.concatenate([summed[:PIECE], summed[PIECE + SLICE :]], axis=0), "far", axis=0)
    parts = spread(jnp.sum(far[:, PIECE:, :], axis=0), group, GROUPS)
    image_far, parts = lax.optimization_barrier((far[:, :PIECE, :], parts))
    image = spread(image_far, group, GROUPS)
    small = lax.all_gather(
        jnp.concatenate([summed[: PIECE + SLICE], jnp.sum(parts, axis=0)], axis=0), col, axis=0
    )
    square = jax.ShapeDtypeStruct((BAND, BAND), f32)
    unit, scaled, left = pl.pallas_call(
        second_kernel,
        out_shape=(square, square, jax.ShapeDtypeStruct((rows, BAND), f32)),
        in_specs=[VMEM] * 2,
        out_specs=(VMEM,) * 3,
        scratch_shapes=[pltpu.VMEM((BAND, 2 * BAND), f32)],
        compiler_params=PARAMS,
        cost_estimate=pl.CostEstimate(flops=10**10, bytes_accessed=2 * 10**6, transcendentals=0),
        name="factorization",
    )(panel, small)
    return pl.pallas_call(
        third_kernel,
        out_shape=jax.ShapeDtypeStruct((rows, width), f32),
        in_specs=[VMEM] * 7,
        out_specs=VMEM,
        scratch_shapes=[pltpu.VMEM((width, BAND), f32)],
        compiler_params=PARAMS,
        name="update",
    )(stored, left, unit, scaled, small, columns, image)


def solution(mesh):
    sizes = (FAR, NEAR, XS, YS, CORES)
    fine_mesh = Mesh(mesh.devices.reshape(sizes), ("far", "near", "x", "y", "core"))
    row, col = ("far", "near", "x"), ("y", "core")
    return jax.shard_map(
        on_device, mesh=fine_mesh, in_specs=(P(row, col), P(row, None)), out_specs=P(row, col), check_vma=False
    )
```

```python
import jax
import jax.numpy as jnp
from jax import lax
from jax.experimental import pallas as pl
from jax.experimental.pallas import tpu as pltpu
from jax.sharding import Mesh, PartitionSpec as P

FINE = 20
BAND = 256
LANES = 128
HALVES = BAND // LANES
TILE = 8
PIECE = FINE * HALVES
SLICE = BAND // 8 * HALVES
FAR, NEAR, XS, YS, CORES = 16, 2, 4, 4, 2
GROUPS = NEAR * XS
COLS = YS * CORES
CHUNKS = 4
NARROW = FAR // CHUNKS
VMEM = pl.BlockSpec(memory_space=pltpu.VMEM)
HBM = pl.BlockSpec(memory_space=pltpu.HBM)
PARAMS = pltpu.CompilerParams(vmem_limit_bytes=48 * 1024 * 1024)


def precise(left, right, dims):
    return lax.dot_general(
        left, right, (dims, ((), ())), precision=lax.Precision.HIGHEST, preferred_element_type=jnp.float32
    )


def identity(n):
    return (lax.broadcasted_iota(jnp.int32, (n, n), 0) == lax.broadcasted_iota(jnp.int32, (n, n), 1)).astype(
        jnp.float32
    )


def split(value):
    high = value.astype(jnp.bfloat16)
    return high, (value - high.astype(jnp.float32)).astype(jnp.bfloat16)


def three_pass(left, right, dims):
    (lh, ll), (rh, rl) = left, right

    def one(a, b):
        return lax.dot_general(a, b, (dims, ((), ())), preferred_element_type=jnp.float32)

    return (one(lh, rl) + one(ll, rh)) + one(lh, rh)


def stack_halves(value):
    return jnp.concatenate([value[:, i * LANES : (i + 1) * LANES] for i in range(HALVES)], axis=0)


def fetch(pieces, landing, arrived, chunk):
    return pltpu.make_async_copy(
        pieces.at[:, pl.ds(chunk * NARROW, NARROW)], landing.at[chunk], arrived.at[chunk]
    )


def assemble(landing, chunk):
    return jnp.concatenate(
        [
            jnp.concatenate(
                [landing[chunk, g, far, half * FINE : (half + 1) * FINE, :] for far in range(NARROW) for g in range(GROUPS)],
                axis=0,
            )
            for half in range(HALVES)
        ],
        axis=1,
    )


def first_kernel(stored, gathered, panel, columns, payload, landing, held, arrived, left):
    wide = NARROW * GROUPS * FINE
    for i in range(CHUNKS):
        fetch(gathered, landing, arrived, i).start()
    image = jnp.zeros((panel.shape[0], BAND), jnp.float32)
    gram = jnp.zeros((BAND, BAND), jnp.float32)
    outgoing = []
    for i in range(CHUNKS):
        fetch(gathered, landing, arrived, i).wait()
        part = assemble(landing, i)
        held[i] = part
        outgoing.append(pltpu.make_async_copy(held.at[i], columns.at[i], left.at[i]))
        outgoing[-1].start()
        image += three_pass(split(stored[:, i * wide : (i + 1) * wide]), split(part), ((1,), (0,)))
        gram += precise(part, part, ((0,), (0,)))
    cross = precise(panel[...], image, ((0,), (0,)))
    eighth = BAND // COLS
    for c in range(COLS):
        payload[c, :PIECE, :] = stack_halves(image[c * FINE : (c + 1) * FINE, :])
        payload[c, PIECE : PIECE + SLICE, :] = stack_halves(gram[c * eighth : (c + 1) * eighth, :])
        payload[c, PIECE + SLICE :, :] = stack_halves(cross[c * eighth : (c + 1) * eighth, :])
    for copy in outgoing:
        copy.wait()


def eliminate(block):
    n, wide = block.shape[0], 2 * block.shape[0]
    eye = identity(n)
    work = jnp.concatenate([block, eye], axis=1)
    tiles = [work[i : i + TILE, :] for i in range(0, n, TILE)]
    sub = lax.broadcasted_iota(jnp.int32, (TILE, wide), 0)
    for t in range(n // TILE):
        j = t * TILE
        rows = [tiles[t][k : k + 1, :] for k in range(TILE)]
        square = [
            [jnp.broadcast_to(rows[k][:, j + l : j + l + 1], (1, wide)) if l >= k else None for l in range(TILE)]
            for k in range(TILE)
        ]
        cols = [[jnp.broadcast_to(tile[:, j + k : j + k + 1], (TILE, wide)) for tile in tiles[t:]] for k in range(TILE)]
        for k in range(TILE):
            inverse = 1.0 / square[k][k]
            for m in range(k + 1, TILE):
                factor = square[k][m] * inverse
                rows[m] = rows[m] - factor * rows[k]
                for l in range(m, TILE):
                    square[m][l] = square[m][l] - factor * square[k][l]
            factors = [col * inverse for col in cols[k]]
            factors[0] = jnp.where(sub > k, factors[0], 0.0)
            for l in range(k + 1, TILE):
                cols[l] = [col - f * square[k][l] for col, f in zip(cols[l], factors)]
            for i, f in enumerate(factors):
                tiles[t + i] = tiles[t + i] - f * rows[k]
    work = jnp.concatenate(tiles, axis=0)
    return work[:, n:], jnp.sum(work[:, :n] * eye, axis=1, keepdims=True)


def invert(gram, work, scaled):
    n, size = 64, BAND
    work[:, :size] = gram
    work[:, size:] = identity(size)
    for k in range(size // n):
        lo, hi = k * n, (k + 1) * n
        unit, pivots = eliminate(work[lo:hi, lo:hi])
        rows = precise(unit, work[lo:hi, lo : size + hi], ((1,), (0,)))
        work[lo:hi, lo : size + hi] = rows
        over = rows * (1.0 / pivots)
        scaled[lo:hi, :] = jnp.zeros((n, size), jnp.float32)
        scaled[lo:hi, :hi] = over[:, size - lo :]
        if hi < size:
            work[hi:, hi : size + hi] = work[hi:, hi : size + hi] - precise(
                rows[:, n : size - lo], over[:, n:], ((0,), (0,))
            )


def unstack(ref, lo, rows):
    return jnp.concatenate(
        [
            jnp.concatenate([ref[c, lo + h * rows : lo + (h + 1) * rows, :] for h in range(HALVES)], axis=1)
            for c in range(COLS)
        ],
        axis=0,
    )


def by_inverse(value, unit, scaled):
    return precise(precise(value, unit, ((1,), (1,))), scaled, ((1,), (0,)))


def second_kernel(panel, small, left, right, work, scaled):
    invert(unstack(small, PIECE, BAND // COLS), work, scaled)
    unit, over = work[:, BAND:], scaled[...]
    first = 2.0 * by_inverse(panel[...], unit, over)
    left[...] = first
    own = unstack(small, 0, FINE)
    cross = unstack(small, PIECE + SLICE, BAND // COLS)
    right[...] = 2.0 * by_inverse(own - precise(first, cross, ((1,), (0,))), unit, over)


def third_kernel(stored, left, right, columns, pieces, out, landing, held, result, arrived, brought, gone):
    wide = NARROW * GROUPS * FINE
    bring = [pltpu.make_async_copy(columns.at[i], held.at[i], brought.at[i]) for i in range(CHUNKS)]
    for i in range(CHUNKS):
        bring[i].start()
        fetch(pieces, landing, arrived, i).start()
    a, b = split(left[...]), split(right[...])
    outgoing = []
    for i in range(CHUNKS):
        at = pl.ds(i * wide, wide)
        bring[i].wait()
        total = three_pass(b, split(held[i]), ((1,), (1,)))
        fetch(pieces, landing, arrived, i).wait()
        total += three_pass(a, split(assemble(landing, i)), ((1,), (1,)))
        result[i] = stored[:, at] - total
        outgoing.append(pltpu.make_async_copy(result.at[i], out.at[:, at], gone.at[i]))
        outgoing[-1].start()
    for copy in outgoing:
        copy.wait()


def copies(value, count):
    return jnp.broadcast_to(value[None], (count, *value.shape))


def spread_kernel(far, out, gone):
    copies = [pltpu.make_async_copy(far.at[:, pl.ds(0, PIECE)], out.at[g], gone.at[g]) for g in range(GROUPS)]
    for copy in copies:
        copy.start()
    for copy in copies:
        copy.wait()


def on_device(stored, panel):
    f32 = jnp.float32
    rows, width = stored.shape
    wide = width // CHUNKS
    col = ("y", "core")
    group = ("near", "x")
    c = lax.axis_index(col)
    semaphores = pltpu.SemaphoreType.DMA((CHUNKS,))
    landing = pltpu.VMEM((CHUNKS, GROUPS, NARROW, PIECE, LANES), f32)
    held = pltpu.VMEM((CHUNKS, wide, BAND), f32)
    own = stack_halves(lax.dynamic_slice_in_dim(panel, c * FINE, FINE, 0))
    gathered = lax.all_to_all(copies(lax.all_gather(own, "far", axis=0), GROUPS), group, 0, 0)
    columns, payload = pl.pallas_call(
        first_kernel,
        out_shape=(
            pltpu.HBM((CHUNKS, wide, BAND), f32),
            jax.ShapeDtypeStruct((COLS, PIECE + 2 * SLICE, LANES), f32),
        ),
        in_specs=[VMEM, HBM, VMEM],
        out_specs=(HBM, VMEM),
        scratch_shapes=[landing, held, semaphores, semaphores],
        compiler_params=PARAMS,
        name="image_and_gram",
    )(stored, gathered, panel)
    summed = jnp.sum(lax.all_to_all(payload, col, 0, 0), axis=0)
    far = lax.all_gather(jnp.concatenate([summed[:PIECE], summed[PIECE + SLICE :]], axis=0), "far", axis=0)
    parts = lax.all_to_all(copies(jnp.sum(far[:, PIECE:, :], axis=0), GROUPS), group, 0, 0)
    image = pl.pallas_call(
        spread_kernel,
        out_shape=pltpu.HBM((GROUPS, FAR, PIECE, LANES), f32),
        in_specs=[VMEM],
        out_specs=HBM,
        scratch_shapes=[pltpu.SemaphoreType.DMA((GROUPS,))],
        compiler_params=PARAMS,
        cost_estimate=pl.CostEstimate(flops=10**10, bytes_accessed=3 * 10**6, transcendentals=0),
        name="image_copies",
    )(far)
    image, parts = lax.optimization_barrier((image, parts))
    image = lax.all_to_all(image, group, 0, 0)
    small = lax.all_gather(
        jnp.concatenate([summed[: PIECE + SLICE], jnp.sum(parts, axis=0)], axis=0), col, axis=0
    )
    left, right = pl.pallas_call(
        second_kernel,
        out_shape=(jax.ShapeDtypeStruct((rows, BAND), f32),) * 2,
        in_specs=[VMEM] * 2,
        out_specs=(VMEM,) * 2,
        scratch_shapes=[pltpu.VMEM((BAND, 2 * BAND), f32), pltpu.VMEM((BAND, BAND), f32)],
        compiler_params=PARAMS,
        cost_estimate=pl.CostEstimate(flops=10**10, bytes_accessed=2 * 10**6, transcendentals=0),
        name="row_factors",
    )(panel, small)
    return pl.pallas_call(
        third_kernel,
        out_shape=jax.ShapeDtypeStruct((rows, width), f32),
        in_specs=[VMEM] * 3 + [HBM] * 2,
        out_specs=HBM,
        scratch_shapes=[landing, held, pltpu.VMEM((CHUNKS, rows, wide), f32)] + [semaphores] * 3,
        compiler_params=PARAMS,
        name="update",
    )(stored, left, right, columns, image)


def solution(mesh):
    sizes = (FAR, NEAR, XS, YS, CORES)
    fine_mesh = Mesh(mesh.devices.reshape(sizes), ("far", "near", "x", "y", "core"))
    row, col = ("far", "near", "x"), ("y", "core")
    return jax.shard_map(
        on_device, mesh=fine_mesh, in_specs=(P(row, col), P(row, None)), out_specs=P(row, col), check_vma=False
    )
```

```python
import jax
import jax.numpy as jnp
from jax import lax
from jax.experimental import pallas as pl
from jax.experimental.pallas import tpu as pltpu
from jax.sharding import Mesh, PartitionSpec as P

FINE = 20
BAND = 256
LANES = 128
HALVES = BAND // LANES
TILE = 8
PIECE = FINE * HALVES
SLICE = BAND // 8 * HALVES
FAR, NEAR, XS, YS, CORES = 16, 2, 4, 4, 2
GROUPS = NEAR * XS
COLS = YS * CORES
CHUNKS = 4
NARROW = FAR // CHUNKS
VMEM = pl.BlockSpec(memory_space=pltpu.VMEM)
HBM = pl.BlockSpec(memory_space=pltpu.HBM)
PARAMS = pltpu.CompilerParams(vmem_limit_bytes=48 * 1024 * 1024)


def precise(left, right, dims):
    return lax.dot_general(
        left, right, (dims, ((), ())), precision=lax.Precision.HIGHEST, preferred_element_type=jnp.float32
    )


def identity(n):
    return (lax.broadcasted_iota(jnp.int32, (n, n), 0) == lax.broadcasted_iota(jnp.int32, (n, n), 1)).astype(
        jnp.float32
    )


def split(value):
    high = value.astype(jnp.bfloat16)
    return high, (value - high.astype(jnp.float32)).astype(jnp.bfloat16)


def one_pass(left, right):
    return lax.dot_general(left, right, (((1,), (0,)), ((), ())), preferred_element_type=jnp.float32)


def three_pass(left, right):
    (lh, ll), (rh, rl) = left, right
    return (one_pass(lh, rl) + one_pass(ll, rh)) + one_pass(lh, rh)


def stack_halves(value):
    return jnp.concatenate([value[:, i * LANES : (i + 1) * LANES] for i in range(HALVES)], axis=0)


def assemble(pieces, chunk):
    fars = range(chunk * NARROW, (chunk + 1) * NARROW)
    return jnp.concatenate(
        [
            jnp.concatenate(
                [pieces[g, far, half * FINE : (half + 1) * FINE, :] for far in fars for g in range(GROUPS)], axis=0
            )
            for half in range(HALVES)
        ],
        axis=1,
    )


def first_kernel(stored, gathered, panel, columns, payload, held, gone):
    f32 = jnp.float32
    wide = NARROW * GROUPS * FINE
    image = jnp.zeros((panel.shape[0], BAND), f32)
    even, odd = jnp.zeros((BAND, BAND), f32), jnp.zeros((BAND, BAND), f32)
    outgoing = []
    for i in range(CHUNKS):
        part = assemble(gathered, i)
        turned = part.T
        held[i] = turned
        outgoing.append(pltpu.make_async_copy(held.at[i], columns.at[i], gone.at[i]))
        outgoing[-1].start()
        high, middle = split(part)
        low = (part - high.astype(f32) - middle.astype(f32)).astype(jnp.bfloat16)
        turned_high, turned_middle = split(turned)
        image += three_pass(split(stored[:, i * wide : (i + 1) * wide]), (high, middle))
        even += one_pass(turned_high, high) + one_pass(turned_middle, middle)
        odd += one_pass(turned_high, middle) + one_pass(turned_high, low)
    gram = even + (odd + odd.T)
    cross = precise(panel[...], image, ((0,), (0,)))
    eighth = BAND // COLS
    for c in range(COLS):
        payload[c, :PIECE, :] = stack_halves(image[c * FINE : (c + 1) * FINE, :])
        payload[c, PIECE : PIECE + SLICE, :] = stack_halves(gram[c * eighth : (c + 1) * eighth, :])
        payload[c, PIECE + SLICE :, :] = stack_halves(cross[c * eighth : (c + 1) * eighth, :])
    for copy in outgoing:
        copy.wait()


def eliminate(block):
    n, wide = block.shape[0], 2 * block.shape[0]
    eye = identity(n)
    work = jnp.concatenate([block, eye], axis=1)
    tiles = [work[i : i + TILE, :] for i in range(0, n, TILE)]
    sub = lax.broadcasted_iota(jnp.int32, (TILE, wide), 0)
    for t in range(n // TILE):
        j = t * TILE
        rows = [tiles[t][k : k + 1, :] for k in range(TILE)]
        square = [
            [jnp.broadcast_to(rows[k][:, j + l : j + l + 1], (1, wide)) if l >= k else None for l in range(TILE)]
            for k in range(TILE)
        ]
        cols = [[jnp.broadcast_to(tile[:, j + k : j + k + 1], (TILE, wide)) for tile in tiles[t:]] for k in range(TILE)]
        for k in range(TILE):
            inverse = 1.0 / square[k][k]
            for m in range(k + 1, TILE):
                factor = square[k][m] * inverse
                rows[m] = rows[m] - factor * rows[k]
                for l in range(m, TILE):
                    square[m][l] = square[m][l] - factor * square[k][l]
            factors = [col * inverse for col in cols[k]]
            factors[0] = jnp.where(sub > k, factors[0], 0.0)
            for l in range(k + 1, TILE):
                cols[l] = [col - f * square[k][l] for col, f in zip(cols[l], factors)]
            for i, f in enumerate(factors):
                tiles[t + i] = tiles[t + i] - f * rows[k]
    work = jnp.concatenate(tiles, axis=0)
    return work[:, n:], jnp.sum(work[:, :n] * eye, axis=1, keepdims=True)


def invert(gram, work, scaled):
    n, size = 64, BAND
    work[:, :size] = gram
    work[:, size:] = identity(size)
    for k in range(size // n):
        lo, hi = k * n, (k + 1) * n
        unit, pivots = eliminate(work[lo:hi, lo:hi])
        rows = precise(unit, work[lo:hi, lo : size + hi], ((1,), (0,)))
        work[lo:hi, lo : size + hi] = rows
        over = rows * (1.0 / pivots)
        scaled[lo:hi, :] = jnp.zeros((n, size), jnp.float32)
        scaled[lo:hi, :hi] = over[:, size - lo :]
        if hi < size:
            work[hi:, hi : size + hi] = work[hi:, hi : size + hi] - precise(
                rows[:, n : size - lo], over[:, n:], ((0,), (0,))
            )


def unstack(ref, lo, rows):
    return jnp.concatenate(
        [
            jnp.concatenate([ref[c, lo + h * rows : lo + (h + 1) * rows, :] for h in range(HALVES)], axis=1)
            for c in range(COLS)
        ],
        axis=0,
    )


def by_inverse(value, unit, scaled):
    return precise(precise(value, unit, ((1,), (1,))), scaled, ((1,), (0,)))


def second_kernel(panel, small, left, right, work, scaled):
    invert(unstack(small, PIECE, BAND // COLS), work, scaled)
    unit, over = work[:, BAND:], scaled[...]
    first = 2.0 * by_inverse(panel[...], unit, over)
    left[...] = first
    own = unstack(small, 0, FINE)
    cross = unstack(small, PIECE + SLICE, BAND // COLS)
    right[...] = 2.0 * by_inverse(own - precise(first, cross, ((1,), (0,))), unit, over)


def third_kernel(stored, left, right, columns, pieces, out, tile, held, result, brought, fetched, gone):
    wide = NARROW * GROUPS * FINE
    parts = [pl.ds(i * wide, wide) for i in range(CHUNKS)]
    bring = [pltpu.make_async_copy(columns.at[i], held.at[i], brought.at[i]) for i in range(CHUNKS)]
    fetch = [pltpu.make_async_copy(stored.at[:, parts[i]], tile.at[i], fetched.at[i]) for i in range(CHUNKS)]
    for copy in bring + fetch:
        copy.start()
    a, b = split(left[...]), split(right[...])
    for i in range(CHUNKS):
        result[i] = three_pass(a, split(assemble(pieces, i).T))
    for copy in bring + fetch:
        copy.wait()
    outgoing = []
    for i in range(CHUNKS):
        result[i] = tile[i] - (result[i] + three_pass(b, split(held[i])))
        outgoing.append(pltpu.make_async_copy(result.at[i], out.at[:, parts[i]], gone.at[i]))
        outgoing[-1].start()
    for copy in outgoing:
        copy.wait()


def in_hbm(value):
    return pltpu.with_memory_space_constraint(value, pltpu.HBM)


def copies(value, count):
    return jnp.broadcast_to(value[None], (count, *value.shape))


def spread_kernel(far, out, gone):
    copies = [pltpu.make_async_copy(far.at[:, pl.ds(0, PIECE)], out.at[g], gone.at[g]) for g in range(GROUPS)]
    for copy in copies:
        copy.start()
    for copy in copies:
        copy.wait()


def on_device(stored, panel):
    f32 = jnp.float32
    rows, width = stored.shape
    wide = width // CHUNKS
    col = ("y", "core")
    group = ("near", "x")
    c = lax.axis_index(col)
    semaphores = pltpu.SemaphoreType.DMA((CHUNKS,))
    held = pltpu.VMEM((CHUNKS, BAND, wide), f32)
    tile = pltpu.VMEM((CHUNKS, rows, wide), f32)
    own = stack_halves(lax.dynamic_slice_in_dim(panel, c * FINE, FINE, 0))
    gathered = lax.all_to_all(copies(lax.all_gather(own, "far", axis=0), GROUPS), group, 0, 0)
    columns, payload = pl.pallas_call(
        first_kernel,
        out_shape=(
            pltpu.HBM((CHUNKS, BAND, wide), f32),
            jax.ShapeDtypeStruct((COLS, PIECE + 2 * SLICE, LANES), f32),
        ),
        in_specs=[VMEM] * 3,
        out_specs=(HBM, VMEM),
        scratch_shapes=[held, semaphores],
        compiler_params=PARAMS,
        name="image_and_gram",
    )(stored, gathered, panel)
    summed = jnp.sum(lax.all_to_all(payload, col, 0, 0), axis=0)
    far = lax.all_gather(jnp.concatenate([summed[:PIECE], summed[PIECE + SLICE :]], axis=0), "far", axis=0)
    parts = lax.all_to_all(copies(jnp.sum(far[:, PIECE:, :], axis=0), GROUPS), group, 0, 0)
    image = pl.pallas_call(
        spread_kernel,
        out_shape=pltpu.HBM((GROUPS, FAR, PIECE, LANES), f32),
        in_specs=[VMEM],
        out_specs=HBM,
        scratch_shapes=[pltpu.SemaphoreType.DMA((GROUPS,))],
        compiler_params=PARAMS,
        cost_estimate=pl.CostEstimate(flops=10**10, bytes_accessed=3 * 10**6, transcendentals=0),
        name="image_copies",
    )(far)
    image, parts = lax.optimization_barrier((image, parts))
    image = lax.all_to_all(image, group, 0, 0)
    small = lax.all_gather(
        jnp.concatenate([summed[: PIECE + SLICE], jnp.sum(parts, axis=0)], axis=0), col, axis=0
    )
    left, right = pl.pallas_call(
        second_kernel,
        out_shape=(jax.ShapeDtypeStruct((rows, BAND), f32),) * 2,
        in_specs=[VMEM] * 2,
        out_specs=(VMEM,) * 2,
        scratch_shapes=[pltpu.VMEM((BAND, 2 * BAND), f32), pltpu.VMEM((BAND, BAND), f32)],
        compiler_params=PARAMS,
        cost_estimate=pl.CostEstimate(flops=10**10, bytes_accessed=2 * 10**6, transcendentals=0),
        name="row_factors",
    )(panel, small)
    return pl.pallas_call(
        third_kernel,
        out_shape=jax.ShapeDtypeStruct((rows, width), f32),
        in_specs=[HBM, VMEM, VMEM, HBM, VMEM],
        out_specs=HBM,
        scratch_shapes=[tile, held, tile] + [semaphores] * 3,
        compiler_params=PARAMS,
        name="update",
    )(in_hbm(stored), left, right, in_hbm(columns), image)


def solution(mesh):
    sizes = (FAR, NEAR, XS, YS, CORES)
    fine_mesh = Mesh(mesh.devices.reshape(sizes), ("far", "near", "x", "y", "core"))
    row, col = ("far", "near", "x"), ("y", "core")
    return jax.shard_map(
        on_device, mesh=fine_mesh, in_specs=(P(row, col), P(row, None)), out_specs=P(row, col), check_vma=False
    )
```

```python
import jax
import jax.numpy as jnp
from jax import lax
from jax.experimental import pallas as pl
from jax.experimental.pallas import tpu as pltpu
from jax.sharding import Mesh, PartitionSpec as P

FINE = 20
BAND = 256
LANES = 128
HALVES = BAND // LANES
TILE = 8
PIECE = FINE * HALVES
FAR, NEAR, XS, YS, CORES = 16, 2, 4, 4, 2
GROUPS = NEAR * XS
COLS = YS * CORES
EIGHTH = BAND // COLS
KEPT = 5
SLICE = EIGHTH * KEPT * EIGHTH // LANES
AXES = ("far", "near", "x", "y", "core")


def neighbours():
    place = [
        [
            [far if near == 0 or core == 0 else (far - 1) % FAR, near, x, y, core]
            for near in range(NEAR)
            for x in range(XS)
        ]
        for far in range(FAR)
        for y in range(YS)
        for core in range(CORES)
    ]

    def index(at):
        far, near, x, y, core = at
        return (((far * NEAR + near) * XS + x) * YS + y) * CORES + core

    return [[index(at) for at in group] for group in place]


CHUNKS = 4
NARROW = FAR // CHUNKS
VMEM = pl.BlockSpec(memory_space=pltpu.VMEM)
HBM = pl.BlockSpec(memory_space=pltpu.HBM)
PARAMS = pltpu.CompilerParams(vmem_limit_bytes=48 * 1024 * 1024)


def precise(left, right, dims):
    return lax.dot_general(
        left, right, (dims, ((), ())), precision=lax.Precision.HIGHEST, preferred_element_type=jnp.float32
    )


def identity(n):
    return (lax.broadcasted_iota(jnp.int32, (n, n), 0) == lax.broadcasted_iota(jnp.int32, (n, n), 1)).astype(
        jnp.float32
    )


def split(value):
    high = value.astype(jnp.bfloat16)
    return high, (value - high.astype(jnp.float32)).astype(jnp.bfloat16)


def one_pass(left, right):
    return lax.dot_general(left, right, (((1,), (0,)), ((), ())), preferred_element_type=jnp.float32)


def three_pass(left, right):
    (lh, ll), (rh, rl) = left, right
    return (one_pass(lh, rl) + one_pass(ll, rh)) + one_pass(lh, rh)


def stack_halves(value):
    return jnp.concatenate([value[:, i * LANES : (i + 1) * LANES] for i in range(HALVES)], axis=0)


def assemble(pieces, chunk):
    fars = range(chunk * NARROW, (chunk + 1) * NARROW)
    return jnp.concatenate(
        [
            jnp.concatenate(
                [pieces[g, far, half * FINE : (half + 1) * FINE, :] for far in fars for g in range(GROUPS)], axis=0
            )
            for half in range(HALVES)
        ],
        axis=1,
    )


def turn(value, by):
    return jnp.concatenate([value[:, by:], value[:, :by]], axis=1) if by else value


def kept_blocks(matrix, c):
    row = turn(matrix[c * EIGHTH : (c + 1) * EIGHTH, :], c * EIGHTH)
    fold = LANES // EIGHTH
    rest = row[:, LANES : KEPT * EIGHTH]
    step = EIGHTH // fold
    return jnp.concatenate(
        [row[:, :LANES], jnp.concatenate([rest[i * step : (i + 1) * step, :] for i in range(fold)], axis=1)], axis=0
    )


def symmetric(ref, lo):
    fold = LANES // EIGHTH
    rows = []
    for c in range(COLS):
        rest = ref[c, lo + EIGHTH : lo + SLICE, :]
        rest = jnp.concatenate([rest[:, i * EIGHTH : (i + 1) * EIGHTH] for i in range(fold)], axis=0)
        empty = jnp.zeros((EIGHTH, BAND - KEPT * EIGHTH), jnp.float32)
        row = jnp.concatenate([ref[c, lo : lo + EIGHTH, :], rest, empty], axis=1)
        rows.append(turn(row, (BAND - c * EIGHTH) % BAND))
    matrix = jnp.concatenate(rows, axis=0)
    row_id = lax.broadcasted_iota(jnp.int32, (BAND, BAND), 0) // EIGHTH
    col_id = lax.broadcasted_iota(jnp.int32, (BAND, BAND), 1) // EIGHTH
    return jnp.where(lax.rem(col_id - row_id + COLS, COLS) < KEPT, matrix, matrix.T)


def first_kernel(stored, gathered, panel, columns, payload, held, gone):
    f32 = jnp.float32
    wide = NARROW * GROUPS * FINE
    image = jnp.zeros((panel.shape[0], BAND), f32)
    even, odd = jnp.zeros((BAND, BAND), f32), jnp.zeros((BAND, BAND), f32)
    outgoing = []
    for i in range(CHUNKS):
        part = assemble(gathered, i)
        turned = part.T
        held[i] = turned
        outgoing.append(pltpu.make_async_copy(held.at[i], columns.at[i], gone.at[i]))
        outgoing[-1].start()
        high, middle = split(part)
        low = (part - high.astype(f32) - middle.astype(f32)).astype(jnp.bfloat16)
        turned_high, turned_middle = split(turned)
        image += three_pass(split(stored[:, i * wide : (i + 1) * wide]), (high, middle))
        even += one_pass(turned_high, high) + one_pass(turned_middle, middle)
        odd += one_pass(turned_high, middle) + one_pass(turned_high, low)
    gram = even + (odd + odd.T)
    cross = precise(panel[...], image, ((0,), (0,)))
    for c in range(COLS):
        payload[c, :PIECE, :] = stack_halves(image[c * FINE : (c + 1) * FINE, :])
        payload[c, PIECE : PIECE + SLICE, :] = kept_blocks(gram, c)
        payload[c, PIECE + SLICE :, :] = kept_blocks(cross, c)
    for copy in outgoing:
        copy.wait()


def eliminate(block):
    n, wide = block.shape[0], 2 * block.shape[0]
    eye = identity(n)
    work = jnp.concatenate([block, eye], axis=1)
    tiles = [work[i : i + TILE, :] for i in range(0, n, TILE)]
    sub = lax.broadcasted_iota(jnp.int32, (TILE, wide), 0)
    for t in range(n // TILE):
        j = t * TILE
        rows = [tiles[t][k : k + 1, :] for k in range(TILE)]
        square = [
            [jnp.broadcast_to(rows[k][:, j + l : j + l + 1], (1, wide)) if l >= k else None for l in range(TILE)]
            for k in range(TILE)
        ]
        cols = [[jnp.broadcast_to(tile[:, j + k : j + k + 1], (TILE, wide)) for tile in tiles[t:]] for k in range(TILE)]
        for k in range(TILE):
            inverse = 1.0 / square[k][k]
            for m in range(k + 1, TILE):
                factor = square[k][m] * inverse
                rows[m] = rows[m] - factor * rows[k]
                for l in range(m, TILE):
                    square[m][l] = square[m][l] - factor * square[k][l]
            factors = [col * inverse for col in cols[k]]
            factors[0] = jnp.where(sub > k, factors[0], 0.0)
            for l in range(k + 1, TILE):
                cols[l] = [col - f * square[k][l] for col, f in zip(cols[l], factors)]
            for i, f in enumerate(factors):
                tiles[t + i] = tiles[t + i] - f * rows[k]
    work = jnp.concatenate(tiles, axis=0)
    return work[:, n:], jnp.sum(work[:, :n] * eye, axis=1, keepdims=True)


def invert(gram, work, scaled):
    n, size = 64, BAND
    work[:, :size] = gram
    work[:, size:] = identity(size)
    for k in range(size // n):
        lo, hi = k * n, (k + 1) * n
        unit, pivots = eliminate(work[lo:hi, lo:hi])
        rows = precise(unit, work[lo:hi, lo : size + hi], ((1,), (0,)))
        work[lo:hi, lo : size + hi] = rows
        over = rows * (1.0 / pivots)
        scaled[lo:hi, :] = jnp.zeros((n, size), jnp.float32)
        scaled[lo:hi, :hi] = over[:, size - lo :]
        if hi < size:
            work[hi:, hi : size + hi] = work[hi:, hi : size + hi] - precise(
                rows[:, n : size - lo], over[:, n:], ((0,), (0,))
            )


def unstack(ref, rows):
    return jnp.concatenate(
        [
            jnp.concatenate([ref[c, h * rows : (h + 1) * rows, :] for h in range(HALVES)], axis=1)
            for c in range(COLS)
        ],
        axis=0,
    )


def by_inverse(value, unit, scaled):
    return precise(precise(value, unit, ((1,), (1,))), scaled, ((1,), (0,)))


def second_kernel(panel, small, left, right, work, scaled):
    invert(symmetric(small, PIECE), work, scaled)
    unit, over = work[:, BAND:], scaled[...]
    first = 2.0 * by_inverse(panel[...], unit, over)
    left[...] = first
    own = unstack(small, FINE)
    cross = symmetric(small, PIECE + SLICE)
    right[...] = 2.0 * by_inverse(own - precise(first, cross, ((1,), (0,))), unit, over)


def third_kernel(stored, left, right, columns, pieces, out, tile, held, result, brought, fetched, gone):
    wide = NARROW * GROUPS * FINE
    parts = [pl.ds(i * wide, wide) for i in range(CHUNKS)]
    bring = [pltpu.make_async_copy(columns.at[i], held.at[i], brought.at[i]) for i in range(CHUNKS)]
    fetch = [pltpu.make_async_copy(stored.at[:, parts[i]], tile.at[i], fetched.at[i]) for i in range(CHUNKS)]
    for copy in bring + fetch:
        copy.start()
    a, b = split(left[...]), split(right[...])
    for i in range(CHUNKS):
        result[i] = three_pass(a, split(assemble(pieces, i).T))
    for copy in bring + fetch:
        copy.wait()
    outgoing = []
    for i in range(CHUNKS):
        result[i] = tile[i] - (result[i] + three_pass(b, split(held[i])))
        outgoing.append(pltpu.make_async_copy(result.at[i], out.at[:, parts[i]], gone.at[i]))
        outgoing[-1].start()
    for copy in outgoing:
        copy.wait()


def in_hbm(value):
    return pltpu.with_memory_space_constraint(value, pltpu.HBM)


def copies(value):
    return jnp.broadcast_to(value[None], (GROUPS, *value.shape))


def exchange(value):
    return lax.all_to_all(value, AXES, 0, 0, axis_index_groups=neighbours())


def spread_kernel(far, out, gone):
    copies = [pltpu.make_async_copy(far.at[:, pl.ds(0, PIECE)], out.at[g], gone.at[g]) for g in range(GROUPS)]
    for copy in copies:
        copy.start()
    for copy in copies:
        copy.wait()


def on_device(stored, panel):
    f32 = jnp.float32
    rows, width = stored.shape
    wide = width // CHUNKS
    col = ("y", "core")
    c = lax.axis_index(col)
    semaphores = pltpu.SemaphoreType.DMA((CHUNKS,))
    held = pltpu.VMEM((CHUNKS, BAND, wide), f32)
    tile = pltpu.VMEM((CHUNKS, rows, wide), f32)
    own = stack_halves(lax.dynamic_slice_in_dim(panel, c * FINE, FINE, 0))
    gathered = exchange(copies(lax.all_gather(own, "far", axis=0)))
    columns, payload = pl.pallas_call(
        first_kernel,
        out_shape=(
            pltpu.HBM((CHUNKS, BAND, wide), f32),
            jax.ShapeDtypeStruct((COLS, PIECE + 2 * SLICE, LANES), f32),
        ),
        in_specs=[VMEM] * 3,
        out_specs=(HBM, VMEM),
        scratch_shapes=[held, semaphores],
        compiler_params=PARAMS,
        name="image_and_gram",
    )(stored, gathered, panel)
    summed = jnp.sum(lax.all_to_all(payload, col, 0, 0), axis=0)
    far = lax.all_gather(jnp.concatenate([summed[:PIECE], summed[PIECE + SLICE :]], axis=0), "far", axis=0)
    parts = exchange(copies(jnp.sum(far[:, PIECE:, :], axis=0)))
    image = pl.pallas_call(
        spread_kernel,
        out_shape=pltpu.HBM((GROUPS, FAR, PIECE, LANES), f32),
        in_specs=[VMEM],
        out_specs=HBM,
        scratch_shapes=[pltpu.SemaphoreType.DMA((GROUPS,))],
        compiler_params=PARAMS,
        cost_estimate=pl.CostEstimate(flops=10**10, bytes_accessed=3 * 10**6, transcendentals=0),
        name="image_copies",
    )(far)
    image, parts = lax.optimization_barrier((image, parts))
    image = exchange(image)
    small = lax.all_gather(
        jnp.concatenate([summed[: PIECE + SLICE], jnp.sum(parts, axis=0)], axis=0), col, axis=0
    )
    left, right = pl.pallas_call(
        second_kernel,
        out_shape=(jax.ShapeDtypeStruct((rows, BAND), f32),) * 2,
        in_specs=[VMEM] * 2,
        out_specs=(VMEM,) * 2,
        scratch_shapes=[pltpu.VMEM((BAND, 2 * BAND), f32), pltpu.VMEM((BAND, BAND), f32)],
        compiler_params=PARAMS,
        cost_estimate=pl.CostEstimate(flops=10**10, bytes_accessed=2 * 10**6, transcendentals=0),
        name="row_factors",
    )(panel, small)
    return pl.pallas_call(
        third_kernel,
        out_shape=jax.ShapeDtypeStruct((rows, width), f32),
        in_specs=[HBM, VMEM, VMEM, HBM, VMEM],
        out_specs=HBM,
        scratch_shapes=[tile, held, tile] + [semaphores] * 3,
        compiler_params=PARAMS,
        name="update",
    )(in_hbm(stored), left, right, in_hbm(columns), image)


def solution(mesh):
    sizes = (FAR, NEAR, XS, YS, CORES)
    fine_mesh = Mesh(mesh.devices.reshape(sizes), AXES)
    row, col = ("far", "near", "x"), ("y", "core")
    return jax.shard_map(
        on_device, mesh=fine_mesh, in_specs=(P(row, col), P(row, None)), out_specs=P(row, col), check_vma=False
    )
```

```python
import jax
import jax.numpy as jnp
from jax import lax
from jax.experimental import pallas as pl
from jax.experimental.pallas import tpu as pltpu
from jax.sharding import Mesh, PartitionSpec as P

FINE = 20
BAND = 256
LANES = 128
HALVES = BAND // LANES
TILE = 8
PIECE = FINE * HALVES
FAR, NEAR, XS, YS, CORES = 16, 2, 4, 4, 2
GROUPS = NEAR * XS
COLS = YS * CORES
EIGHTH = BAND // COLS
KEPT = 5
SLICE = EIGHTH * KEPT * EIGHTH // LANES
AXES = ("far", "near", "x", "y", "core")
CHUNKS = 4
NARROW = FAR // CHUNKS
VMEM = pl.BlockSpec(memory_space=pltpu.VMEM)
HBM = pl.BlockSpec(memory_space=pltpu.HBM)
PARAMS = pltpu.CompilerParams(vmem_limit_bytes=48 * 1024 * 1024)


def precise(left, right, dims):
    return lax.dot_general(
        left, right, (dims, ((), ())), precision=lax.Precision.HIGHEST, preferred_element_type=jnp.float32
    )


def identity(n):
    return (lax.broadcasted_iota(jnp.int32, (n, n), 0) == lax.broadcasted_iota(jnp.int32, (n, n), 1)).astype(
        jnp.float32
    )


def split(value):
    high = value.astype(jnp.bfloat16)
    return high, (value - high.astype(jnp.float32)).astype(jnp.bfloat16)


def one_pass(left, right):
    return lax.dot_general(left, right, (((1,), (0,)), ((), ())), preferred_element_type=jnp.float32)


def three_pass(left, right):
    (lh, ll), (rh, rl) = left, right
    return (one_pass(lh, rl) + one_pass(ll, rh)) + one_pass(lh, rh)


def stack_halves(value):
    return jnp.concatenate([value[:, i * LANES : (i + 1) * LANES] for i in range(HALVES)], axis=0)


def assemble(pieces, chunk):
    fars = range(chunk * NARROW, (chunk + 1) * NARROW)
    return jnp.concatenate(
        [
            jnp.concatenate(
                [pieces[g, far, half * FINE : (half + 1) * FINE, :] for far in fars for g in range(GROUPS)], axis=0
            )
            for half in range(HALVES)
        ],
        axis=1,
    )


def turn(value, by):
    return jnp.concatenate([value[:, by:], value[:, :by]], axis=1) if by else value


def kept_blocks(matrix, c):
    row = turn(matrix[c * EIGHTH : (c + 1) * EIGHTH, :], c * EIGHTH)
    fold = LANES // EIGHTH
    rest = row[:, LANES : KEPT * EIGHTH]
    step = EIGHTH // fold
    return jnp.concatenate(
        [row[:, :LANES], jnp.concatenate([rest[i * step : (i + 1) * step, :] for i in range(fold)], axis=1)], axis=0
    )


def symmetric(ref, lo):
    fold = LANES // EIGHTH
    rows = []
    for c in range(COLS):
        rest = ref[c, lo + EIGHTH : lo + SLICE, :]
        rest = jnp.concatenate([rest[:, i * EIGHTH : (i + 1) * EIGHTH] for i in range(fold)], axis=0)
        empty = jnp.zeros((EIGHTH, BAND - KEPT * EIGHTH), jnp.float32)
        row = jnp.concatenate([ref[c, lo : lo + EIGHTH, :], rest, empty], axis=1)
        rows.append(turn(row, (BAND - c * EIGHTH) % BAND))
    matrix = jnp.concatenate(rows, axis=0)
    row_id = lax.broadcasted_iota(jnp.int32, (BAND, BAND), 0) // EIGHTH
    col_id = lax.broadcasted_iota(jnp.int32, (BAND, BAND), 1) // EIGHTH
    return jnp.where(lax.rem(col_id - row_id + COLS, COLS) < KEPT, matrix, matrix.T)


def first_kernel(stored, gathered, panel, columns, payload, held, gone):
    f32 = jnp.float32
    wide = NARROW * GROUPS * FINE
    image = jnp.zeros((panel.shape[0], BAND), f32)
    even, odd = jnp.zeros((BAND, BAND), f32), jnp.zeros((BAND, BAND), f32)
    outgoing = []
    for i in range(CHUNKS):
        part = assemble(gathered, i)
        turned = part.T
        held[i] = turned
        outgoing.append(pltpu.make_async_copy(held.at[i], columns.at[i], gone.at[i]))
        outgoing[-1].start()
        high, middle = split(part)
        low = (part - high.astype(f32) - middle.astype(f32)).astype(jnp.bfloat16)
        turned_high, turned_middle = split(turned)
        image += three_pass(split(stored[:, i * wide : (i + 1) * wide]), (high, middle))
        even += one_pass(turned_high, high) + one_pass(turned_middle, middle)
        odd += one_pass(turned_high, middle) + one_pass(turned_high, low)
    gram = even + (odd + odd.T)
    cross = precise(panel[...], image, ((0,), (0,)))
    for c in range(COLS):
        payload[c, :PIECE, :] = stack_halves(image[c * FINE : (c + 1) * FINE, :])
        payload[c, PIECE : PIECE + SLICE, :] = kept_blocks(gram, c)
        payload[c, PIECE + SLICE :, :] = kept_blocks(cross, c)
    for copy in outgoing:
        copy.wait()


def eliminate(block):
    n, wide = block.shape[0], 2 * block.shape[0]
    eye = identity(n)
    work = jnp.concatenate([block, eye], axis=1)
    tiles = [work[i : i + TILE, :] for i in range(0, n, TILE)]
    sub = lax.broadcasted_iota(jnp.int32, (TILE, wide), 0)
    for t in range(n // TILE):
        j = t * TILE
        rows = [tiles[t][k : k + 1, :] for k in range(TILE)]
        square = [
            [jnp.broadcast_to(rows[k][:, j + l : j + l + 1], (1, wide)) if l >= k else None for l in range(TILE)]
            for k in range(TILE)
        ]
        cols = [[jnp.broadcast_to(tile[:, j + k : j + k + 1], (TILE, wide)) for tile in tiles[t:]] for k in range(TILE)]
        for k in range(TILE):
            inverse = 1.0 / square[k][k]
            for m in range(k + 1, TILE):
                factor = square[k][m] * inverse
                rows[m] = rows[m] - factor * rows[k]
                for l in range(m, TILE):
                    square[m][l] = square[m][l] - factor * square[k][l]
            factors = [col * inverse for col in cols[k]]
            factors[0] = jnp.where(sub > k, factors[0], 0.0)
            for l in range(k + 1, TILE):
                cols[l] = [col - f * square[k][l] for col, f in zip(cols[l], factors)]
            for i, f in enumerate(factors):
                tiles[t + i] = tiles[t + i] - f * rows[k]
    work = jnp.concatenate(tiles, axis=0)
    return work[:, n:], jnp.sum(work[:, :n] * eye, axis=1, keepdims=True)


def invert(gram, work, scaled):
    n, size = 64, BAND
    work[:, :size] = gram
    work[:, size:] = identity(size)
    for k in range(size // n):
        lo, hi = k * n, (k + 1) * n
        unit, pivots = eliminate(work[lo:hi, lo:hi])
        rows = precise(unit, work[lo:hi, lo : size + hi], ((1,), (0,)))
        work[lo:hi, lo : size + hi] = rows
        over = rows * (1.0 / pivots)
        scaled[lo:hi, :] = jnp.zeros((n, size), jnp.float32)
        scaled[lo:hi, :hi] = over[:, size - lo :]
        if hi < size:
            work[hi:, hi : size + hi] = work[hi:, hi : size + hi] - precise(
                rows[:, n : size - lo], over[:, n:], ((0,), (0,))
            )


def unstack(ref, rows):
    return jnp.concatenate(
        [
            jnp.concatenate([ref[c, h * rows : (h + 1) * rows, :] for h in range(HALVES)], axis=1)
            for c in range(COLS)
        ],
        axis=0,
    )


def by_inverse(value, unit, scaled):
    return precise(precise(value, unit, ((1,), (1,))), scaled, ((1,), (0,)))


def second_kernel(panel, small, left, right, work, scaled):
    invert(symmetric(small, PIECE), work, scaled)
    unit, over = work[:, BAND:], scaled[...]
    first = 2.0 * by_inverse(panel[...], unit, over)
    left[...] = first
    own = unstack(small, FINE)
    cross = symmetric(small, PIECE + SLICE)
    right[...] = 2.0 * by_inverse(own - precise(first, cross, ((1,), (0,))), unit, over)


def third_kernel(stored, left, right, columns, pieces, out, tile, held, result, brought, fetched, gone):
    wide = NARROW * GROUPS * FINE
    parts = [pl.ds(i * wide, wide) for i in range(CHUNKS)]
    bring = [pltpu.make_async_copy(columns.at[i], held.at[i], brought.at[i]) for i in range(CHUNKS)]
    fetch = [pltpu.make_async_copy(stored.at[:, parts[i]], tile.at[i], fetched.at[i]) for i in range(CHUNKS)]
    for copy in bring + fetch:
        copy.start()
    a, b = split(left[...]), split(right[...])
    for i in range(CHUNKS):
        result[i] = three_pass(a, split(assemble(pieces, i).T))
    for copy in bring + fetch:
        copy.wait()
    outgoing = []
    for i in range(CHUNKS):
        result[i] = tile[i] - (result[i] + three_pass(b, split(held[i])))
        outgoing.append(pltpu.make_async_copy(result.at[i], out.at[:, parts[i]], gone.at[i]))
        outgoing[-1].start()
    for copy in outgoing:
        copy.wait()


def in_hbm(value):
    return pltpu.with_memory_space_constraint(value, pltpu.HBM)


def copies(value):
    return jnp.broadcast_to(value[None], (GROUPS, *value.shape))


def exchange(value):
    return lax.all_to_all(value, ("near", "x"), 0, 0)


def spread_kernel(far, out, gone):
    copies = [pltpu.make_async_copy(far.at[:, pl.ds(0, PIECE)], out.at[g], gone.at[g]) for g in range(GROUPS)]
    for copy in copies:
        copy.start()
    for copy in copies:
        copy.wait()


def on_device(stored, panel):
    f32 = jnp.float32
    rows, width = stored.shape
    wide = width // CHUNKS
    col = ("y", "core")
    c = lax.axis_index(col)
    semaphores = pltpu.SemaphoreType.DMA((CHUNKS,))
    held = pltpu.VMEM((CHUNKS, BAND, wide), f32)
    tile = pltpu.VMEM((CHUNKS, rows, wide), f32)
    own = stack_halves(lax.dynamic_slice_in_dim(panel, c * FINE, FINE, 0))
    gathered = exchange(copies(lax.all_gather(own, "far", axis=0)))
    columns, payload = pl.pallas_call(
        first_kernel,
        out_shape=(
            pltpu.HBM((CHUNKS, BAND, wide), f32),
            jax.ShapeDtypeStruct((COLS, PIECE + 2 * SLICE, LANES), f32),
        ),
        in_specs=[VMEM] * 3,
        out_specs=(HBM, VMEM),
        scratch_shapes=[held, semaphores],
        compiler_params=PARAMS,
        name="image_and_gram",
    )(stored, gathered, panel)
    summed = jnp.sum(lax.all_to_all(payload, col, 0, 0), axis=0)
    far = lax.all_gather(jnp.concatenate([summed[:PIECE], summed[PIECE + SLICE :]], axis=0), "far", axis=0)
    parts = exchange(copies(jnp.sum(far[:, PIECE:, :], axis=0)))
    image = pl.pallas_call(
        spread_kernel,
        out_shape=pltpu.HBM((GROUPS, FAR, PIECE, LANES), f32),
        in_specs=[VMEM],
        out_specs=HBM,
        scratch_shapes=[pltpu.SemaphoreType.DMA((GROUPS,))],
        compiler_params=PARAMS,
        cost_estimate=pl.CostEstimate(flops=10**10, bytes_accessed=3 * 10**6, transcendentals=0),
        name="image_copies",
    )(far)
    image, parts = lax.optimization_barrier((image, parts))
    image = exchange(image)
    small = lax.all_gather(
        jnp.concatenate([summed[: PIECE + SLICE], jnp.sum(parts, axis=0)], axis=0), col, axis=0
    )
    left, right = pl.pallas_call(
        second_kernel,
        out_shape=(jax.ShapeDtypeStruct((rows, BAND), f32),) * 2,
        in_specs=[VMEM] * 2,
        out_specs=(VMEM,) * 2,
        scratch_shapes=[pltpu.VMEM((BAND, 2 * BAND), f32), pltpu.VMEM((BAND, BAND), f32)],
        compiler_params=PARAMS,
        cost_estimate=pl.CostEstimate(flops=10**10, bytes_accessed=2 * 10**6, transcendentals=0),
        name="row_factors",
    )(panel, small)
    return pl.pallas_call(
        third_kernel,
        out_shape=jax.ShapeDtypeStruct((rows, width), f32),
        in_specs=[HBM, VMEM, VMEM, HBM, VMEM],
        out_specs=HBM,
        scratch_shapes=[tile, held, tile] + [semaphores] * 3,
        compiler_params=PARAMS,
        name="update",
    )(in_hbm(stored), left, right, in_hbm(columns), image)


def solution(mesh):
    sizes = (FAR, NEAR, XS, YS, CORES)
    fine_mesh = Mesh(mesh.devices.reshape(sizes), AXES)
    row, col = ("far", "near", "x"), ("y", "core")
    return jax.shard_map(
        on_device, mesh=fine_mesh, in_specs=(P(row, col), P(row, None)), out_specs=P(row, col), check_vma=False
    )
```

```python
import jax
import jax.numpy as jnp
from jax import lax
from jax.experimental import pallas as pl
from jax.experimental.pallas import tpu as pltpu
from jax.sharding import Mesh, PartitionSpec as P

FINE = 20
BAND = 256
LANES = 128
HALVES = BAND // LANES
TILE = 8
PIECE = FINE * HALVES
FAR, NEAR, XS, YS, CORES = 16, 2, 4, 4, 2
GROUPS = NEAR * XS
COLS = YS * CORES
EIGHTH = BAND // COLS
KEPT = 5
SLICE = EIGHTH * KEPT * EIGHTH // LANES
SPARE = 24
AXES = ("far", "near", "x", "y", "core")
CHUNKS = 4
NARROW = FAR // CHUNKS
VMEM = pl.BlockSpec(memory_space=pltpu.VMEM)
HBM = pl.BlockSpec(memory_space=pltpu.HBM)
PARAMS = pltpu.CompilerParams(vmem_limit_bytes=48 * 1024 * 1024)


def precise(left, right, dims):
    return lax.dot_general(
        left, right, (dims, ((), ())), precision=lax.Precision.HIGHEST, preferred_element_type=jnp.float32
    )


def identity(n):
    return (lax.broadcasted_iota(jnp.int32, (n, n), 0) == lax.broadcasted_iota(jnp.int32, (n, n), 1)).astype(
        jnp.float32
    )


def split(value):
    high = value.astype(jnp.bfloat16)
    return high, (value - high.astype(jnp.float32)).astype(jnp.bfloat16)


def one_pass(left, right):
    return lax.dot_general(left, right, (((1,), (0,)), ((), ())), preferred_element_type=jnp.float32)


def three_pass(left, right):
    (lh, ll), (rh, rl) = left, right
    return (one_pass(lh, rl) + one_pass(ll, rh)) + one_pass(lh, rh)


def stack_halves(value):
    return jnp.concatenate([value[:, i * LANES : (i + 1) * LANES] for i in range(HALVES)], axis=0)


def assemble(pieces, chunk):
    fars = range(chunk * NARROW, (chunk + 1) * NARROW)
    return jnp.concatenate(
        [
            jnp.concatenate(
                [pieces[g, far, half * FINE : (half + 1) * FINE, :] for far in fars for g in range(GROUPS)], axis=0
            )
            for half in range(HALVES)
        ],
        axis=1,
    )


def turn(value, by):
    return jnp.concatenate([value[:, by:], value[:, :by]], axis=1) if by else value


def kept_blocks(matrix, c):
    row = turn(matrix[c * EIGHTH : (c + 1) * EIGHTH, :], c * EIGHTH)
    fold = LANES // EIGHTH
    rest = row[:, LANES : KEPT * EIGHTH]
    step = EIGHTH // fold
    return jnp.concatenate(
        [row[:, :LANES], jnp.concatenate([rest[i * step : (i + 1) * step, :] for i in range(fold)], axis=1)], axis=0
    )


def symmetric(ref, lo):
    fold = LANES // EIGHTH
    rows = []
    for c in range(COLS):
        rest = ref[c, lo + EIGHTH : lo + SLICE, :]
        rest = jnp.concatenate([rest[:, i * EIGHTH : (i + 1) * EIGHTH] for i in range(fold)], axis=0)
        empty = jnp.zeros((EIGHTH, BAND - KEPT * EIGHTH), jnp.float32)
        row = jnp.concatenate([ref[c, lo : lo + EIGHTH, :], rest, empty], axis=1)
        rows.append(turn(row, (BAND - c * EIGHTH) % BAND))
    matrix = jnp.concatenate(rows, axis=0)
    row_id = lax.broadcasted_iota(jnp.int32, (BAND, BAND), 0) // EIGHTH
    col_id = lax.broadcasted_iota(jnp.int32, (BAND, BAND), 1) // EIGHTH
    return jnp.where(lax.rem(col_id - row_id + COLS, COLS) < KEPT, matrix, matrix.T)


def first_kernel(stored, gathered, panel, columns, payload, held, gone):
    f32 = jnp.float32
    wide = NARROW * GROUPS * FINE
    image = jnp.zeros((panel.shape[0], BAND), f32)
    even, odd = jnp.zeros((BAND, BAND), f32), jnp.zeros((BAND, BAND), f32)
    outgoing = []
    for i in range(CHUNKS):
        part = assemble(gathered, i)
        turned = part.T
        held[i] = turned
        outgoing.append(pltpu.make_async_copy(held.at[i], columns.at[i], gone.at[i]))
        outgoing[-1].start()
        high, middle = split(part)
        low = (part - high.astype(f32) - middle.astype(f32)).astype(jnp.bfloat16)
        turned_high, turned_middle = split(turned)
        image += three_pass(split(stored[:, i * wide : (i + 1) * wide]), (high, middle))
        even += one_pass(turned_high, high) + one_pass(turned_middle, middle)
        odd += one_pass(turned_high, middle) + one_pass(turned_high, low)
    gram = even + (odd + odd.T)
    cross = precise(panel[...], image, ((0,), (0,)))
    for c in range(COLS):
        payload[c, :PIECE, :] = stack_halves(image[c * FINE : (c + 1) * FINE, :])
        payload[c, PIECE : PIECE + SLICE, :] = kept_blocks(gram, c)
        payload[c, PIECE + SLICE :, :] = kept_blocks(cross, c)
    for copy in outgoing:
        copy.wait()


def eliminate(block):
    n, wide = block.shape[0], 2 * block.shape[0]
    eye = identity(n)
    work = jnp.concatenate([block, eye], axis=1)
    tiles = [work[i : i + TILE, :] for i in range(0, n, TILE)]
    sub = lax.broadcasted_iota(jnp.int32, (TILE, wide), 0)
    for t in range(n // TILE):
        j = t * TILE
        rows = [tiles[t][k : k + 1, :] for k in range(TILE)]
        square = [
            [jnp.broadcast_to(rows[k][:, j + l : j + l + 1], (1, wide)) if l >= k else None for l in range(TILE)]
            for k in range(TILE)
        ]
        cols = [[jnp.broadcast_to(tile[:, j + k : j + k + 1], (TILE, wide)) for tile in tiles[t:]] for k in range(TILE)]
        for k in range(TILE):
            inverse = 1.0 / square[k][k]
            for m in range(k + 1, TILE):
                factor = square[k][m] * inverse
                rows[m] = rows[m] - factor * rows[k]
                for l in range(m, TILE):
                    square[m][l] = square[m][l] - factor * square[k][l]
            factors = [col * inverse for col in cols[k]]
            factors[0] = jnp.where(sub > k, factors[0], 0.0)
            for l in range(k + 1, TILE):
                cols[l] = [col - f * square[k][l] for col, f in zip(cols[l], factors)]
            for i, f in enumerate(factors):
                tiles[t + i] = tiles[t + i] - f * rows[k]
    work = jnp.concatenate(tiles, axis=0)
    return work[:, n:], jnp.sum(work[:, :n] * eye, axis=1, keepdims=True)


def invert(gram, work, scaled):
    n, size = 64, BAND
    work[:, :size] = gram
    work[:, size:] = identity(size)
    for k in range(size // n):
        lo, hi = k * n, (k + 1) * n
        unit, pivots = eliminate(work[lo:hi, lo:hi])
        rows = precise(unit, work[lo:hi, lo : size + hi], ((1,), (0,)))
        work[lo:hi, lo : size + hi] = rows
        over = rows * (1.0 / pivots)
        scaled[lo:hi, :] = jnp.zeros((n, size), jnp.float32)
        scaled[lo:hi, :hi] = over[:, size - lo :]
        if hi < size:
            work[hi:, hi : size + hi] = work[hi:, hi : size + hi] - precise(
                rows[:, n : size - lo], over[:, n:], ((0,), (0,))
            )


def unstack(ref, rows):
    return jnp.concatenate(
        [
            jnp.concatenate([ref[c, h * rows : (h + 1) * rows, :] for h in range(HALVES)], axis=1)
            for c in range(COLS)
        ],
        axis=0,
    )


def by_inverse(value, unit, scaled):
    return precise(precise(value, unit, ((1,), (1,))), scaled, ((1,), (0,)))


def second_kernel(panel, small, left, right, work, scaled):
    invert(symmetric(small, PIECE), work, scaled)
    unit, over = work[:, BAND:], scaled[...]
    first = 2.0 * by_inverse(panel[...], unit, over)
    left[...] = first
    own = unstack(small, FINE)
    cross = symmetric(small, PIECE + SLICE)
    right[...] = 2.0 * by_inverse(own - precise(first, cross, ((1,), (0,))), unit, over)


def third_kernel(stored, left, right, columns, pieces, out, tile, held, result, brought, fetched, gone):
    wide = NARROW * GROUPS * FINE
    parts = [pl.ds(i * wide, wide) for i in range(CHUNKS)]
    bring = [pltpu.make_async_copy(columns.at[i], held.at[i], brought.at[i]) for i in range(CHUNKS)]
    fetch = [pltpu.make_async_copy(stored.at[:, parts[i]], tile.at[i], fetched.at[i]) for i in range(CHUNKS)]
    for copy in bring + fetch:
        copy.start()
    a, b = split(left[...]), split(right[...])
    for i in range(CHUNKS):
        result[i] = three_pass(a, split(assemble(pieces, i).T))
    for copy in bring + fetch:
        copy.wait()
    outgoing = []
    for i in range(CHUNKS):
        result[i] = tile[i] - (result[i] + three_pass(b, split(held[i])))
        outgoing.append(pltpu.make_async_copy(result.at[i], out.at[:, parts[i]], gone.at[i]))
        outgoing[-1].start()
    for copy in outgoing:
        copy.wait()


def in_hbm(value):
    return pltpu.with_memory_space_constraint(value, pltpu.HBM)


def copies(value):
    return jnp.broadcast_to(value[None], (GROUPS, *value.shape))


def exchange(value):
    return lax.all_to_all(value, ("near", "x"), 0, 0)


def spread_kernel(far, out, gone):
    copies = [pltpu.make_async_copy(far.at[:, pl.ds(0, PIECE)], out.at[g], gone.at[g]) for g in range(GROUPS)]
    for copy in copies:
        copy.start()
    for copy in copies:
        copy.wait()


def on_device(stored, panel):
    f32 = jnp.float32
    rows, width = stored.shape
    wide = width // CHUNKS
    col = ("y", "core")
    c = lax.axis_index(col)
    semaphores = pltpu.SemaphoreType.DMA((CHUNKS,))
    held = pltpu.VMEM((CHUNKS, BAND, wide), f32)
    tile = pltpu.VMEM((CHUNKS, rows, wide), f32)
    own = stack_halves(lax.dynamic_slice_in_dim(panel, c * FINE, FINE, 0))
    gathered = exchange(copies(lax.all_gather(own, "far", axis=0)))
    columns, payload = pl.pallas_call(
        first_kernel,
        out_shape=(
            pltpu.HBM((CHUNKS, BAND, wide), f32),
            jax.ShapeDtypeStruct((COLS, PIECE + 2 * SLICE, LANES), f32),
        ),
        in_specs=[VMEM] * 3,
        out_specs=(HBM, VMEM),
        scratch_shapes=[held, semaphores],
        compiler_params=PARAMS,
        name="image_and_gram",
    )(stored, gathered, panel)
    summed = jnp.sum(lax.all_to_all(payload, col, 0, 0), axis=0)
    spare = jnp.zeros((SPARE, LANES), f32)
    far = lax.all_gather(jnp.concatenate([summed[:PIECE], summed[PIECE + SLICE :], spare], axis=0), "far", axis=0)
    parts = exchange(copies(jnp.sum(far[:, PIECE : PIECE + SLICE, :], axis=0)))
    image = pl.pallas_call(
        spread_kernel,
        out_shape=pltpu.HBM((GROUPS, FAR, PIECE, LANES), f32),
        in_specs=[VMEM],
        out_specs=HBM,
        scratch_shapes=[pltpu.SemaphoreType.DMA((GROUPS,))],
        compiler_params=PARAMS,
        cost_estimate=pl.CostEstimate(flops=10**10, bytes_accessed=3 * 10**6, transcendentals=0),
        name="image_copies",
    )(far)
    image, parts = lax.optimization_barrier((image, parts))
    image = exchange(image)
    small = lax.all_gather(
        jnp.concatenate([summed[: PIECE + SLICE], jnp.sum(parts, axis=0)], axis=0), col, axis=0
    )
    left, right = pl.pallas_call(
        second_kernel,
        out_shape=(jax.ShapeDtypeStruct((rows, BAND), f32),) * 2,
        in_specs=[VMEM] * 2,
        out_specs=(VMEM,) * 2,
        scratch_shapes=[pltpu.VMEM((BAND, 2 * BAND), f32), pltpu.VMEM((BAND, BAND), f32)],
        compiler_params=PARAMS,
        cost_estimate=pl.CostEstimate(flops=10**10, bytes_accessed=2 * 10**6, transcendentals=0),
        name="row_factors",
    )(panel, small)
    return pl.pallas_call(
        third_kernel,
        out_shape=jax.ShapeDtypeStruct((rows, width), f32),
        in_specs=[HBM, VMEM, VMEM, HBM, VMEM],
        out_specs=HBM,
        scratch_shapes=[tile, held, tile] + [semaphores] * 3,
        compiler_params=PARAMS,
        name="update",
    )(in_hbm(stored), left, right, in_hbm(columns), image)


def solution(mesh):
    sizes = (FAR, NEAR, XS, YS, CORES)
    fine_mesh = Mesh(mesh.devices.reshape(sizes), AXES)
    row, col = ("far", "near", "x"), ("y", "core")
    return jax.shard_map(
        on_device, mesh=fine_mesh, in_specs=(P(row, col), P(row, None)), out_specs=P(row, col), check_vma=False
    )
```
